256 devices in a mesh: ctx: 32 (over z_lo, x, core), head: 8 (over z_hi, y).
Axes of the slice: x: 4, y: 4, z: 8 (z_hi: 2, z_lo: 4; z = z_hi * 4 + z_lo), core: 2. Of those that a mesh axis runs over, the one named last changes fastest.
Arguments:
- rotated_query_rows: bfloat16 [32768, 4096], P(('ctx', 'head')), may hold values from -6.5 to 6.5
- rotated_key_rows: bfloat16 [32768, 1024], P(('ctx', 'head')), may hold values from -4 to 4
- value_row_matrix: bfloat16 [32768, 1024], P(('ctx', 'head')), may hold values from -5 to 5
- vert_blocks: int32 [8, 512, 8], P('head', 'ctx'), may hold values from -1 to 495, as said below
- slash_offsets: int32 [8, 512, 4], P('head', 'ctx'), may hold values from -1 to 15, as said below
- out_weight: bfloat16 [4096, 4096], P('head'), may hold values from -0.09375 to 0.09375
- residual: bfloat16 [32768, 4096], P(('ctx', 'head')), may hold values from -0.29882812 to 0.29882812
- norm_gain: bfloat16 [4096], replicated, may hold values from 0.5 to 1.5
Outputs:
- hidden_out: bfloat16 [32768, 4096], P(('ctx', 'head'))
- normed: bfloat16 [32768, 4096], P(('ctx', 'head'))
The draws below stay inside these ranges and needn't reach their ends.
Inputs may be any that keep to these rules, and one draw needn't show every extreme that they name: `vert_blocks`: for query block i and key-value head h: -1 marks an empty entry; the other entries are distinct key blocks; block 0 is listed when i >= 16, block i - 16 when i > 16, and the others lie in 1 to i - 16. `slash_offsets`: for query block i: the first entry is 0; the others are -1 or distinct offsets of 1 to min(15, i).
All inputs are finite; a program needn't handle non-finite values.
Results may differ from the reference program's by a relative error of at most 0.017.
Values may be sent and summed in bfloat16 or wider, within the bound.
A program may use at most 128 MiB of HBM per device.

```python
import jax
import jax.numpy as jnp
from jax import lax

D = 4096
QUERY_HEADS = 32
KEY_VALUE_HEADS = 8
HEAD_SIZE = 128
MASK_BLOCK_SIZE = 64
NV = 8
NS = 4
SLASH_REACH = 16
WINDOW_TOKENS = 32768
QUERY_BLOCK_COUNT = 512
N_HEAD = 8


def draw_rotated_query_rows(key, part):
    starting_key = jax.random.fold_in(key, 1)
    value_entries = jnp.clip(jax.random.normal(starting_key, (WINDOW_TOKENS, D)), -4.0, 4.0)
    return value_entries.astype(jnp.bfloat16)


def draw_rotated_key_rows(key, part):
    starting_key = jax.random.fold_in(key, 2)
    value_entries = jnp.clip(jax.random.normal(starting_key, (WINDOW_TOKENS, KEY_VALUE_HEADS * HEAD_SIZE)), -4.0, 4.0)
    return value_entries.astype(jnp.bfloat16)


def draw_vert_blocks(key, part):
    local_key_block = jax.random.fold_in(key, 11)
    block_location = jnp.arange(QUERY_BLOCK_COUNT, dtype=jnp.int32)[:, None]
    columns = jnp.arange(QUERY_BLOCK_COUNT, dtype=jnp.int32)[None, :]
    unprocessed_input = jax.random.randint(local_key_block, (KEY_VALUE_HEADS, QUERY_BLOCK_COUNT, QUERY_BLOCK_COUNT), 0, 1 << 20)
    valid = (columns >= 1) & (columns <= block_location - SLASH_REACH)
    score = jnp.where(valid, unprocessed_input * QUERY_BLOCK_COUNT + columns, (1 << 30) + columns)
    score = jnp.where(valid & (columns == block_location - SLASH_REACH), -1, score)
    order = jnp.argsort(score, axis=-1)[..., :NV - 1].astype(jnp.int32)
    count = jnp.maximum(block_location - SLASH_REACH, 0)
    slot = jnp.arange(NV - 1, dtype=jnp.int32)[None, :]
    picked = jnp.where(slot < count, order, -1)
    leading_entry = jnp.broadcast_to(jnp.where(block_location >= SLASH_REACH, 0, -1), (KEY_VALUE_HEADS, QUERY_BLOCK_COUNT, 1)).astype(jnp.int32)
    return jnp.concatenate([leading_entry, picked.astype(jnp.int32)], axis=-1)


def draw_slash_offsets(key, part):
    local_key_block = jax.random.fold_in(key, 12)
    block_location = jnp.arange(QUERY_BLOCK_COUNT, dtype=jnp.int32)[:, None]
    offsets = jnp.arange(SLASH_REACH, dtype=jnp.int32)[None, :]
    unprocessed_input = jax.random.randint(local_key_block, (KEY_VALUE_HEADS, QUERY_BLOCK_COUNT, SLASH_REACH), 0, 1 << 20)
    valid = (offsets >= 1) & (offsets <= block_location)
    score = jnp.where(valid, unprocessed_input * SLASH_REACH + offsets, (1 << 30) + offsets)
    order = jnp.argsort(score, axis=-1)[..., :NS - 1].astype(jnp.int32)
    count = jnp.minimum(block_location, SLASH_REACH - 1)
    slot = jnp.arange(NS - 1, dtype=jnp.int32)[None, :]
    picked = jnp.where(slot < count, order, -1)
    leading_entry = jnp.zeros((KEY_VALUE_HEADS, QUERY_BLOCK_COUNT, 1), jnp.int32)
    return jnp.concatenate([leading_entry, picked.astype(jnp.int32)], axis=-1)


def block_levels(own_key, dims, pieces, least, largest):
    def one(dim, blocks):
        steps = jax.random.uniform(jax.random.fold_in(jax.random.fold_in(own_key, 6), dim), (blocks,), jnp.float32, least / len(pieces), largest / len(pieces))
        return jnp.repeat(jnp.exp(steps), dims[dim] // blocks).reshape((-1,) + (1,) * (len(dims) - dim - 1))

    gain = one(*pieces[0])
    for cut in pieces[1:]:
        gain = gain * one(*cut)
    return gain


def scatter_about(stream_key, extent, deviation, reach, pieces=(), kind=jnp.bfloat16):
    result = jax.random.normal(stream_key, extent, jnp.float32) * deviation
    if len(pieces) > 0:
        result = block_levels(stream_key, extent, pieces, -0.22, 0.18) * result
    return jnp.clip(result, min=-reach, max=reach).astype(kind)


def setup_inputs(seed: int = 0) -> dict:
    arg_keys = jax.random.split(jax.random.key(seed), 9)
    return {
        "rotated_query_rows": draw_rotated_query_rows(jax.random.fold_in(arg_keys[8], 71), 0),
        "rotated_key_rows": draw_rotated_key_rows(jax.random.fold_in(arg_keys[8], 71), 0),
        "value_row_matrix": scatter_about(arg_keys[2], (WINDOW_TOKENS, KEY_VALUE_HEADS * HEAD_SIZE), 1.0, 5.0, ((0, 256),)),
        "vert_blocks": draw_vert_blocks(jax.random.fold_in(arg_keys[8], 71), 0),
        "slash_offsets": draw_slash_offsets(jax.random.fold_in(arg_keys[8], 71), 0),
        "out_weight": scatter_about(arg_keys[5], (D, D), D ** -0.5, 0.09375, ((0, 8),)),
        "residual": scatter_about(arg_keys[6], (WINDOW_TOKENS, D), 0.05, 0.29882812, ((0, 256),)),
        "norm_gain": jnp.clip(1.0 + 0.1 * jax.random.normal(arg_keys[7], (D,), jnp.float32), 0.5, 1.5).astype(jnp.bfloat16),
    }


def attend_head(query_blocks, key_head, value_head, vert_list, slash_list, block_ids):
    count_blocks = query_blocks.shape[0]
    slash_blocks = jnp.where(slash_list >= 0, block_ids[:, None] - slash_list, -1).astype(jnp.int32)
    listed = jnp.concatenate([vert_list, slash_blocks], axis=1)
    present = listed >= 0
    clamped = jnp.maximum(listed, 0).astype(jnp.int32)
    offsets = jnp.arange(MASK_BLOCK_SIZE, dtype=jnp.int32)
    key_rows = (clamped[:, :, None] * MASK_BLOCK_SIZE + offsets[None, None, :]).reshape(count_blocks, -1)
    key_sel = key_head[key_rows]
    value_sel = value_head[key_rows]
    query_pos = block_ids[:, None] * MASK_BLOCK_SIZE + offsets[None, :]
    allowed = jnp.repeat(present, MASK_BLOCK_SIZE, axis=1)[:, None, :] & (key_rows[:, None, :] <= query_pos[:, :, None])
    scores = jnp.einsum('nbgd,nkd->ngbk', query_blocks.astype(jnp.float32), key_sel.astype(jnp.float32)) * HEAD_SIZE ** (-0.5)
    scores = jnp.where(allowed[:, None, :, :], scores, -1e+30)
    row_max = lax.optimization_barrier(jnp.max(scores, axis=-1, keepdims=True))
    weights = jnp.where(allowed[:, None, :, :], jnp.exp(scores - row_max), 0.0)
    total = lax.optimization_barrier(jnp.sum(weights, axis=-1))
    weights_b = weights.astype(jnp.bfloat16)
    mixed = jnp.einsum('ngbk,nkd->ngbd', weights_b.astype(jnp.float32), value_sel.astype(jnp.float32))
    mixed = mixed / total[..., None]
    return jnp.transpose(mixed, (0, 2, 1, 3)).astype(jnp.bfloat16)

def reference(rotated_query_rows, rotated_key_rows, value_row_matrix, vert_blocks, slash_offsets, out_weight, residual, norm_gain):
    head_group = QUERY_HEADS // KEY_VALUE_HEADS
    full_query_rows = jnp.transpose(rotated_query_rows.reshape(QUERY_BLOCK_COUNT, MASK_BLOCK_SIZE, KEY_VALUE_HEADS, head_group, HEAD_SIZE), (2, 0, 1, 3, 4))
    full_key_rows = jnp.transpose(rotated_key_rows.reshape(WINDOW_TOKENS, KEY_VALUE_HEADS, HEAD_SIZE), (1, 0, 2))
    full_value_rows = jnp.transpose(value_row_matrix.reshape(WINDOW_TOKENS, KEY_VALUE_HEADS, HEAD_SIZE), (1, 0, 2))
    block_ids = jnp.arange(QUERY_BLOCK_COUNT, dtype=jnp.int32)

    def per_head(items):
        return attend_head(items[0], items[1], items[2], items[3], items[4], block_ids)
    heads_out = lax.map(per_head, (full_query_rows, full_key_rows, full_value_rows, vert_blocks, slash_offsets))
    attn = jnp.transpose(heads_out, (1, 2, 0, 3, 4)).reshape(WINDOW_TOKENS, D)
    width_part = D // N_HEAD
    proj = jnp.zeros((WINDOW_TOKENS, D), jnp.float32)
    for group_pos in range(N_HEAD):
        part = jnp.dot(attn[:, group_pos * width_part:(group_pos + 1) * width_part], out_weight[group_pos * width_part:(group_pos + 1) * width_part], preferred_element_type=jnp.float32).astype(jnp.bfloat16)
        proj = proj + part.astype(jnp.float32)
    stream = residual.astype(jnp.float32) + proj
    hidden_out = stream.astype(jnp.bfloat16)
    mean_square = lax.optimization_barrier(jnp.mean(stream * stream, axis=-1, keepdims=True))
    normed = (stream * lax.rsqrt(mean_square + 1e-05) * norm_gain.astype(jnp.float32)).astype(jnp.bfloat16)
    return (hidden_out, normed)
```

```python
import functools

import jax
import jax.numpy as jnp
from jax import lax
from jax.experimental import pallas as pl
from jax.experimental.pallas import tpu as pltpu
from jax.sharding import PartitionSpec as P

MESH = pl.DeviceIdType.MESH
HEAD_SIZE = 128
MASK_BLOCK_SIZE = 64
LANES = 128
GROUP = 4
NV = 8
NS = 4
RING = 4
HEADS = 8
CHUNKS = 4
D = 4096
CHUNK = D // CHUNKS
NEGATIVE = -1e30
EXPONENT_SCALE = HEAD_SIZE**-0.5 * 1.4426950408889634


def kernel(
    q_in, k_in, v_in, w_in, vert, slash, residual, gain,
    hidden_out, normed_out,
    kv, queries, weight, mixed, gathered, outgoing, incoming, stream,
    head_send, head_recv, query_send, query_recv, z_send, z_recv,
    right_send, right_recv, left_send, left_recv, core_send, core_recv,
    wright_send, wright_recv, wleft_send, wleft_recv, wcore_send, wcore_recv,
    mix_send, mix_recv, part_send, part_recv, local_sem,
):
    ctx = lax.axis_index("ctx")
    head = lax.axis_index("head")
    core, x, row = ctx % 2, (ctx // 2) % RING, ctx // (2 * RING)
    y, half = head % RING, head // RING

    def at_ctx(row_, x_, core_):
        return ((row_ * RING + x_) * 2 + core_, head)

    right = at_ctx(row, (x + 1) % RING, core)
    left = at_ctx(row, (x + 3) % RING, core)
    other_core = at_ctx(row, x, 1 - core)
    up = at_ctx((row + 1) % RING, x, core)
    down = at_ctx((row + 3) % RING, x, core)
    y_right = (ctx, half * RING + (y + 1) % RING)
    y_left = (ctx, half * RING + (y + 3) % RING)
    partner = (ctx, (1 - half) * RING + y)

    def head_peer(j):
        return (ctx, (head + j) % HEADS)

    def remote(src, dst, send, recv, device):
        return pltpu.make_async_remote_copy(
            src_ref=src, dst_ref=dst, send_sem=send, recv_sem=recv,
            device_id=device, device_id_type=MESH,
        )

    def landed(dst, recv):
        remote(dst, dst, recv, recv, other_core).wait_recv()

    def sent(src, send):
        remote(src, src, send, send, other_core).wait_send()

    barrier = pltpu.get_barrier_semaphore()
    friends = [head_peer(j) for j in range(1, HEADS)] + [right, left, other_core, up, down]
    for friend in friends:
        pl.semaphore_signal(barrier, inc=1, device_id=friend, device_id_type=MESH)

    def own_rows(n):
        return pltpu.make_async_copy(
            (k_in, v_in)[n].at[:, :, pl.ds(pl.multiple_of(head * LANES, LANES), LANES)],
            kv.at[n, pl.ds(ctx * 16 + head * 2, 2)],
            local_sem.at[n],
        )

    def own_queries():
        return pltpu.make_async_copy(
            q_in.at[:, pl.ds(pl.multiple_of(head * 512, 512), 512)],
            queries.at[head],
            local_sem.at[2],
        )

    def own_weight(n):
        return pltpu.make_async_copy(
            w_in.at[:, pl.ds(n * CHUNK, CHUNK)], weight.at[n, y], local_sem.at[3 + n]
        )

    own_rows(0).start()
    own_rows(1).start()
    pl.semaphore_wait(barrier, len(friends))

    def head_copy(j, n):
        peer = head_peer(j)
        src = (k_in, v_in)[n]
        return remote(
            src.at[:, :, pl.ds(pl.multiple_of(peer[1] * LANES, LANES), LANES)],
            kv.at[n, pl.ds(ctx * 16 + head * 2, 2)],
            head_send.at[n, j], head_recv.at[n, j], peer,
        )

    def query_copy(j):
        peer = head_peer(j)
        return remote(
            q_in.at[:, pl.ds(pl.multiple_of(peer[1] * 512, 512), 512)],
            queries.at[head],
            query_send.at[j], query_recv.at[j], peer,
        )

    for j in (4, 3, 5, 2, 6, 1, 7):
        for n in range(2):
            head_copy(j, n).start()
    for n in range(2):
        own_rows(n).wait()
    for j in range(1, HEADS):
        source = (head + HEADS - j) % HEADS
        for n in range(2):
            landed(kv.at[n, pl.ds(ctx * 16 + source * 2, 2)], head_recv.at[n, j])

    def piece(row_, x_, core_):
        return pl.ds(((row_ * RING + x_) * 2 + core_) * 16, 16)

    def half_rows(start, count):
        return pl.ds(pl.multiple_of(core * 256 + start, 128), count)

    def weight_first(n, direction):
        rows = half_rows(0, 256)
        src = w_in.at[rows, pl.ds(n * CHUNK, CHUNK)]
        dst = weight.at[n, y, rows]
        if direction > 0:
            return remote(src, dst, wright_send.at[n, 0], wright_recv.at[n, 0], y_right)
        return remote(src, dst, wleft_send.at[n, 0], wleft_recv.at[n, 0], y_left)

    def ctx_step(s):
        row_s = row - s
        own = kv.at[:, piece(row_s, x, core)]

        @pl.when(s > 0)
        def _():
            landed(own, z_recv.at[s])

        @pl.when(row < RING - 1)
        def _():
            remote(own, own, z_send.at[s], z_recv.at[s + 1], up).start()

        for n in (0, 1):
            part = kv.at[n, piece(row_s, x, core)]
            remote(part, part, right_send.at[s, n], right_recv.at[s, n], right).start()
            part = kv.at[1 - n, piece(row_s, x, core)]
            remote(part, part, left_send.at[s, 1 - n], left_recv.at[s, 1 - n], left).start()
        remote(own, own, core_send.at[s, 0], core_recv.at[s, 0], other_core).start()

        @pl.when(s > 0)
        def _():
            opposite(s - 1)

        @pl.when(s == 0)
        def _():
            for j in (4, 3, 5, 2, 6, 1, 7):
                query_copy(j).start()
            own_queries().start()
            for n in range(CHUNKS):
                own_weight(n).start()
                weight_first(n, 1).start()
                weight_first(n, -1).start()

        from_left = piece(row_s, (x + 3) % RING, core)
        from_right = piece(row_s, (x + 1) % RING, core)
        part = kv.at[0, from_left]
        landed(part, right_recv.at[s, 0])
        remote(part, part, right_send.at[s, 2], right_recv.at[s, 2], right).start()
        part = kv.at[1, from_right]
        landed(part, left_recv.at[s, 1])
        remote(part, part, left_send.at[s, 2], left_recv.at[s, 2], left).start()
        landed(kv.at[1, from_left], right_recv.at[s, 1])
        part = kv.at[:, from_left]
        remote(part, part, core_send.at[s, 1], core_recv.at[s, 1], other_core).start()
        landed(kv.at[0, from_right], left_recv.at[s, 0])
        part = kv.at[:, from_right]
        remote(part, part, core_send.at[s, 2], core_recv.at[s, 2], other_core).start()

    def opposite(s):
        far = piece(row - s, (x + 2) % RING, core)
        landed(kv.at[0, far], right_recv.at[s, 2])
        landed(kv.at[1, far], left_recv.at[s, 2])
        part = kv.at[:, far]
        remote(part, part, core_send.at[s, 3], core_recv.at[s, 3], other_core).start()

    def core_landed(s):
        for n, shift in enumerate((0, 3, 1, 2)):
            landed(kv.at[:, piece(row - s, (x + shift) % RING, 1 - core)], core_recv.at[s, n])

    def weight_step(n):
        from_left, from_right = (y + 3) % RING, (y + 1) % RING
        rows, low, high = half_rows(0, 256), half_rows(0, 128), half_rows(128, 128)
        landed(weight.at[n, from_left, rows], wright_recv.at[n, 0])
        part = weight.at[n, from_left, low]
        remote(part, part, wright_send.at[n, 1], wright_recv.at[n, 1], y_right).start()
        landed(weight.at[n, from_right, rows], wleft_recv.at[n, 0])
        part = weight.at[n, from_right, high]
        remote(part, part, wleft_send.at[n, 1], wleft_recv.at[n, 1], y_left).start()
        for m, source in enumerate((from_left, from_right)):
            part = weight.at[n, source, rows]
            remote(part, part, wcore_send.at[n, m], wcore_recv.at[n, m], other_core).start()

    def weight_far(n):
        far = (y + 2) % RING
        landed(weight.at[n, far, half_rows(0, 128)], wright_recv.at[n, 1])
        landed(weight.at[n, far, half_rows(128, 128)], wleft_recv.at[n, 1])
        part = weight.at[n, far, half_rows(0, 256)]
        remote(part, part, wcore_send.at[n, 2], wcore_recv.at[n, 2], other_core).start()

    def weight_landed(n):
        rows = pl.ds(pl.multiple_of((1 - core) * 256, 256), 256)
        for m, shift in enumerate((3, 1, 2)):
            landed(weight.at[n, (y + shift) % RING, rows], wcore_recv.at[n, m])

    lane = lax.broadcasted_iota(jnp.int32, (1, LANES), 1)
    diagonal_row = lax.broadcasted_iota(jnp.int32, (GROUP * MASK_BLOCK_SIZE, LANES), 0) % MASK_BLOCK_SIZE
    diagonal_lane = lax.broadcasted_iota(jnp.int32, (GROUP * MASK_BLOCK_SIZE, LANES), 1)
    future = (diagonal_lane < MASK_BLOCK_SIZE) & (diagonal_lane > diagonal_row)

    def attend(pair, b):
        block = pair * 2 + b
        blocks, biases = [], []
        for j in range(NV):
            entry = vert[0, j, block]
            blocks.append(jnp.maximum(entry, 0))
            biases.append(jnp.where(entry >= 0, 0.0, NEGATIVE).astype(jnp.float32))
        for j in range(NS):
            entry = slash[0, j, block]
            blocks.append(ctx * 16 + block - jnp.maximum(entry, 0))
            biases.append(jnp.where(entry >= 0, 0.0, NEGATIVE).astype(jnp.float32))
        rows = pl.ds(b * MASK_BLOCK_SIZE, MASK_BLOCK_SIZE)
        query = jnp.concatenate(
            [queries[pair, rows, pl.ds(g * HEAD_SIZE, HEAD_SIZE)] for g in range(GROUP)], axis=0
        )
        keys = jnp.concatenate([kv[0, n] for n in blocks], axis=0)
        scores = lax.dot_general(
            query, keys, (((1,), (1,)), ((), ())), preferred_element_type=jnp.float32
        )
        pieces = []
        for n in range((NV + NS) // 2):
            bias = jnp.where(lane < MASK_BLOCK_SIZE, biases[2 * n], biases[2 * n + 1])
            part = scores[:, n * LANES : (n + 1) * LANES] + bias
            if n == NV // 2:
                part = jnp.where(future, NEGATIVE, part)
            pieces.append(part)
        scores = jnp.concatenate(pieces, axis=1)
        top = jnp.max(scores, axis=-1, keepdims=True)
        weights = jnp.exp2((scores - top) * EXPONENT_SCALE)
        total = jnp.sum(weights, axis=-1, keepdims=True)
        values = jnp.concatenate([kv[1, n] for n in blocks], axis=0)
        out = jnp.dot(weights.astype(jnp.bfloat16), values, preferred_element_type=jnp.float32)
        out = (out / total).astype(jnp.bfloat16)
        for g in range(GROUP):
            mixed[pair, rows, pl.ds(g * HEAD_SIZE, HEAD_SIZE)] = out[
                g * MASK_BLOCK_SIZE : (g + 1) * MASK_BLOCK_SIZE
            ]

    def mix_place(m):
        turn, j = m // RING, m % RING + 1
        token_half = (1 - half) * (1 - turn) + half * turn
        return turn, j, token_half, (y + j) % RING

    def attention():
        lax.fori_loop(0, row + 1, lambda s, carry: (core_landed(s), carry)[1], 0)
        own_queries().wait()
        for j in range(1, HEADS):
            landed(queries.at[(head + HEADS - j) % HEADS], query_recv.at[j])

        def pair_step(m, carry):
            turn, j, token_half, target = mix_place(m)
            pair = token_half * RING + target
            for b in range(2):
                attend(pair, b)

            @pl.when(j < RING)
            def _():
                remote(
                    mixed.at[pair], gathered.at[token_half, y],
                    mix_send.at[m], mix_recv.at[m], (ctx, half * RING + target),
                ).start()

            @pl.when(j == RING)
            def _():
                gathered[token_half, y] = mixed[pair]

            return carry

        lax.fori_loop(0, 2 * RING, pair_step, 0)

    def mix_landed(turn):
        token_half = 1 - half if turn == 0 else half
        for j in range(1, RING):
            landed(gathered.at[token_half, (y + RING - j) % RING], mix_recv.at[turn * RING + j - 1])

    def project(token_half, n, columns):
        total = None
        for source in range(RING):
            term = jnp.dot(
                gathered[token_half, source], weight[n, source, :, columns],
                preferred_element_type=jnp.float32,
            )
            total = term if total is None else total + term
        return total

    def send_part(n, carry):
        weight_landed(n)
        for t in range(CHUNK // 512):
            columns = pl.ds(t * 512, 512)
            outgoing[n, :, columns] = project(1 - half, n, columns).astype(jnp.bfloat16)
        remote(
            outgoing.at[n], incoming.at[n], part_send.at[n], part_recv.at[n], partner
        ).start()
        return carry

    def step(s, carry):
        @pl.when(s <= row)
        def _():
            ctx_step(s)

        @pl.when(s < CHUNKS)
        def _():
            weight_step(s)

        @pl.when(s == row)
        def _():
            opposite(s)
            attention()

        @pl.when(s > 0)
        def _():
            weight_far(s - 1)

        @pl.when(s == row + 1)
        def _():
            for n in range(CHUNKS):
                own_weight(n).wait()
            mix_landed(0)

        first = jnp.where(s == row + 1, 0, s - 1)
        last = jnp.where(s > row, s, first)
        lax.fori_loop(first, last, send_part, 0)
        return carry

    lax.fori_loop(0, CHUNKS + 1, step, 0)

    mix_landed(1)

    def own_part(n, carry):
        for t in range(CHUNK // 512):
            columns = pl.ds(t * 512, 512)
            stream[n, :, columns] = project(half, n, columns)
        return carry

    lax.fori_loop(0, CHUNKS, own_part, 0)

    square = jnp.zeros((128, 1), jnp.float32)
    for n in range(CHUNKS):
        landed(incoming.at[n], part_recv.at[n])
        columns = slice(n * CHUNK, (n + 1) * CHUNK)
        value = (
            residual[:, columns].astype(jnp.float32)
            + stream[n]
            + incoming[n].astype(jnp.float32)
        )
        stream[n] = value
        hidden_out[:, columns] = value.astype(jnp.bfloat16)
        square = square + jnp.sum(value * value, axis=-1, keepdims=True)
    scale = lax.rsqrt(square * (1.0 / D) + 1e-05)
    for n in range(D // LANES):
        place = n * LANES % CHUNK
        value = stream[n * LANES // CHUNK, :, place : place + LANES]
        normed_out[:, n * LANES : (n + 1) * LANES] = (
            value * scale * gain[n : n + 1].astype(jnp.float32)
        ).astype(jnp.bfloat16)

    for j in range(1, HEADS):
        for n in range(2):
            head_copy(j, n).wait_send()
        query_copy(j).wait_send()

    def ctx_sent(s, carry):
        own = kv.at[:, piece(row - s, x, core)]

        @pl.when(row < RING - 1)
        def _():
            sent(own, z_send.at[s])

        for n in range(3):
            part = kv.at[0, piece(row - s, x, core)]
            sent(part, right_send.at[s, n])
            sent(part, left_send.at[s, n])
        for n in range(4):
            sent(own, core_send.at[s, n])
        return carry

    lax.fori_loop(0, row + 1, ctx_sent, 0)

    def weight_sent(n, carry):
        rows, low = half_rows(0, 256), half_rows(0, 128)
        sent(weight.at[n, y, rows], wright_send.at[n, 0])
        sent(weight.at[n, y, rows], wleft_send.at[n, 0])
        sent(weight.at[n, y, low], wright_send.at[n, 1])
        sent(weight.at[n, y, low], wleft_send.at[n, 1])
        for m in range(3):
            sent(weight.at[n, y, rows], wcore_send.at[n, m])
        sent(outgoing.at[n], part_send.at[n])
        return carry

    lax.fori_loop(0, CHUNKS, weight_sent, 0)
    for turn in range(2):
        for j in range(1, RING):
            sent(mixed.at[0], mix_send.at[turn * RING + j - 1])


def per_device(q, k, v, vert, slash, out_weight, residual, norm_gain):
    anywhere = pl.BlockSpec(memory_space=pl.ANY)
    vmem = pl.BlockSpec(memory_space=pltpu.VMEM)
    smem = pl.BlockSpec(memory_space=pltpu.SMEM)
    dma = pltpu.SemaphoreType.DMA
    tokens = q.shape[0]
    return pl.pallas_call(
        kernel,
        out_shape=[jax.ShapeDtypeStruct((tokens, D), jnp.bfloat16)] * 2,
        in_specs=[anywhere] * 4 + [smem, smem, vmem, vmem],
        out_specs=[vmem, vmem],
        scratch_shapes=[
            pltpu.VMEM((2, 512, MASK_BLOCK_SIZE, HEAD_SIZE), jnp.bfloat16),
            pltpu.VMEM((HEADS, tokens, 512), jnp.bfloat16),
            pltpu.VMEM((CHUNKS, RING, 512, CHUNK), jnp.bfloat16),
            pltpu.VMEM((HEADS, tokens, 512), jnp.bfloat16),
            pltpu.VMEM((2, RING, tokens, 512), jnp.bfloat16),
            pltpu.VMEM((CHUNKS, tokens, CHUNK), jnp.bfloat16),
            pltpu.VMEM((CHUNKS, tokens, CHUNK), jnp.bfloat16),
            pltpu.VMEM((CHUNKS, tokens, CHUNK), jnp.float32),
            dma((2, HEADS)), dma((2, HEADS)), dma((HEADS,)), dma((HEADS,)),
            dma((RING,)), dma((RING,)),
            dma((RING, 3)), dma((RING, 3)), dma((RING, 3)), dma((RING, 3)),
            dma((RING, 4)), dma((RING, 4)),
            dma((CHUNKS, 2)), dma((CHUNKS, 2)), dma((CHUNKS, 2)), dma((CHUNKS, 2)),
            dma((CHUNKS, 3)), dma((CHUNKS, 3)),
            dma((2 * RING,)), dma((2 * RING,)), dma((CHUNKS,)), dma((CHUNKS,)),
            dma((3 + CHUNKS,)),
        ],
        compiler_params=pltpu.CompilerParams(
            collective_id=0, has_side_effects=True, vmem_limit_bytes=58 * 1024 * 1024
        ),
        cost_estimate=pl.CostEstimate(
            flops=6_000_000_000, bytes_accessed=10_000_000, transcendentals=3_200_000
        ),
        name="attention_layer",
    )(
        q,
        k.reshape(tokens // MASK_BLOCK_SIZE, MASK_BLOCK_SIZE, -1),
        v.reshape(tokens // MASK_BLOCK_SIZE, MASK_BLOCK_SIZE, -1),
        out_weight, vert.transpose(0, 2, 1), slash.transpose(0, 2, 1), residual,
        norm_gain.reshape(D // LANES, LANES),
    )


def solution(mesh):
    token_rows = P(("ctx", "head"), None)
    return jax.shard_map(
        lambda *args: tuple(per_device(*args)),
        mesh=mesh,
        in_specs=(
            token_rows, token_rows, token_rows,
            P("head", "ctx", None), P("head", "ctx", None),
            P("head", None), token_rows, P(),
        ),
        out_specs=(token_rows, token_rows),
        check_vma=False,
    )
```

```python
import functools

import jax
import jax.numpy as jnp
from jax import lax
from jax.experimental import pallas as pl
from jax.experimental.pallas import tpu as pltpu
from jax.sharding import PartitionSpec as P

MESH = pl.DeviceIdType.MESH
HEAD_SIZE = 128
MASK_BLOCK_SIZE = 64
LANES = 128
GROUP = 4
NV = 8
NS = 4
RING = 4
HEADS = 8
CHUNKS = 4
D = 4096
CHUNK = D // CHUNKS
NEGATIVE = -1e30
EXPONENT_SCALE = HEAD_SIZE**-0.5 * 1.4426950408889634


def kernel(
    q_in, k_in, v_in, w_in, vert, slash,
    stream,
    kv, queries, weight, mixed, gathered, outgoing, incoming,
    near_send, near_recv, far_send, far_recv, query_send, query_recv,
    up_send, up_recv, down_send, down_recv,
    right_send, right_recv, left_send, left_recv, core_send, core_recv,
    wright_send, wright_recv, wleft_send, wleft_recv, wcore_send, wcore_recv,
    mix_send, mix_recv, part_send, part_recv, local_sem,
):
    ctx = lax.axis_index("ctx")
    head = lax.axis_index("head")
    core, x, row = ctx % 2, (ctx // 2) % RING, ctx // (2 * RING)
    y, half = head % RING, head // RING

    def at_ctx(row_, x_, core_):
        return ((row_ * RING + x_) * 2 + core_, head)

    right = at_ctx(row, (x + 1) % RING, core)
    left = at_ctx(row, (x + 3) % RING, core)
    other_core = at_ctx(row, x, 1 - core)
    up = at_ctx((row + 1) % RING, x, core)
    down = at_ctx((row + 3) % RING, x, core)
    y_right = (ctx, half * RING + (y + 1) % RING)
    y_left = (ctx, half * RING + (y + 3) % RING)
    partner = (ctx, (1 - half) * RING + y)

    def head_peer(j):
        return (ctx, (head + j) % HEADS)

    def remote(src, dst, send, recv, device):
        return pltpu.make_async_remote_copy(
            src_ref=src, dst_ref=dst, send_sem=send, recv_sem=recv,
            device_id=device, device_id_type=MESH,
        )

    def landed(dst, recv):
        remote(dst, dst, recv, recv, other_core).wait_recv()

    def sent(src, send):
        remote(src, src, send, send, other_core).wait_send()

    def far_peer(row_, y_):
        return ((row_ * RING + x) * 2 + core, (1 - half) * RING + y_)

    barrier = pltpu.get_barrier_semaphore()
    friends = [head_peer(j) for j in range(1, HEADS)] + [right, left, other_core, up, down]
    for friend in friends:
        pl.semaphore_signal(barrier, inc=1, device_id=friend, device_id_type=MESH)

    @pl.when(row == RING - 1)
    def _():
        for row_ in range(RING - 1):
            for y_ in range(RING):
                pl.semaphore_signal(
                    barrier, inc=1, device_id=far_peer(row_, y_), device_id_type=MESH
                )

    def own_rows(n):
        return pltpu.make_async_copy(
            (k_in, v_in)[n].at[:, :, pl.ds(pl.multiple_of(head * LANES, LANES), LANES)],
            kv.at[n, pl.ds(ctx * 16 + head * 2, 2)],
            local_sem.at[n],
        )

    def own_queries():
        return pltpu.make_async_copy(
            q_in.at[:, pl.ds(pl.multiple_of(head * 512, 512), 512)],
            queries.at[head],
            local_sem.at[2],
        )

    def own_weight(n):
        return pltpu.make_async_copy(
            w_in.at[:, pl.ds(n * CHUNK, CHUNK)], weight.at[n, y], local_sem.at[3 + n]
        )

    own_rows(0).start()
    own_rows(1).start()
    pl.semaphore_wait(barrier, len(friends) + jnp.where(row < RING - 1, RING, 0))

    def key_value_copy(n, target, send, recv, device):
        src = (k_in, v_in)[n]
        return remote(
            src.at[:, :, pl.ds(pl.multiple_of(target * LANES, LANES), LANES)],
            kv.at[n, pl.ds(ctx * 16 + head * 2, 2)], send, recv, device,
        )

    def near_copy(j, n):
        target = half * RING + (y + j) % RING
        return key_value_copy(n, target, near_send.at[j, n], near_recv.at[j, n], (ctx, target))

    def far_copy(j, n):
        y_ = (y + j) % RING
        device = far_peer(RING - 1, y_)
        return key_value_copy(
            n, device[1], far_send.at[j, n], far_recv.at[row, j, n], device
        )

    def query_copy(j):
        peer = head_peer(j)
        return remote(
            q_in.at[:, pl.ds(pl.multiple_of(peer[1] * 512, 512), 512)],
            queries.at[head],
            query_send.at[j], query_recv.at[j], peer,
        )

    for j in (1, 3, 2):
        for n in range(2):
            near_copy(j, n).start()
    for j in range(RING):
        for n in range(2):
            far_copy(j, n).start()

    def piece(row_, x_, core_, u):
        owner = half if u == 0 else 1 - half
        return pl.ds(((row_ * RING + x_) * 2 + core_) * 16 + owner * 8, 8)

    def far_landed(row_):
        @pl.when(row == RING - 1)
        def _():
            for j in range(RING):
                source = (1 - half) * RING + (y + RING - j) % RING
                place = pl.ds(((row_ * RING + x) * 2 + core) * 16 + source * 2, 2)
                for n in range(2):
                    landed(kv.at[n, place], far_recv.at[row_, j, n])

        @pl.when(row < RING - 1)
        def _():
            landed(kv.at[:, piece(row_, x, core, 1)], down_recv.at[row_])

    def hand_down(row_, carry):
        far_landed(row_)
        part = kv.at[:, piece(row_, x, core, 1)]
        remote(part, part, down_send.at[row_], down_recv.at[row_], down).start()
        return carry

    def half_rows(start, count):
        return pl.ds(pl.multiple_of(core * 256 + start, 128), count)

    def weight_first(n):
        rows = half_rows(0, 256)
        src = w_in.at[rows, pl.ds(n * CHUNK, CHUNK)]
        dst = weight.at[n, y, rows]
        remote(src, dst, wright_send.at[n, 0], wright_recv.at[n, 0], y_right).start()
        remote(src, dst, wleft_send.at[n, 0], wleft_recv.at[n, 0], y_left).start()

    for n in range(CHUNKS):
        weight_first(n)

    def ctx_step(s, u):
        row_s = row - s
        q = u * RING + s
        own = kv.at[:, piece(row_s, x, core, u)]
        if u == 0:
            @pl.when(s == 0)
            def _():
                for n in range(2):
                    own_rows(n).wait()
                for j in range(1, RING):
                    source = half * RING + (y + RING - j) % RING
                    for n in range(2):
                        landed(kv.at[n, pl.ds(ctx * 16 + source * 2, 2)], near_recv.at[j, n])

            @pl.when(s > 0)
            def _():
                landed(own, up_recv.at[s])

            @pl.when(row < RING - 1)
            def _():
                remote(own, own, up_send.at[s], up_recv.at[s + 1], up).start()
        else:
            @pl.when(s == 0)
            def _():
                far_landed(row)

        for n in (0, 1):
            part = kv.at[n, piece(row_s, x, core, u)]
            remote(part, part, right_send.at[q, n], right_recv.at[q, n], right).start()
            part = kv.at[1 - n, piece(row_s, x, core, u)]
            remote(part, part, left_send.at[q, 1 - n], left_recv.at[q, 1 - n], left).start()
        remote(own, own, core_send.at[q, 0], core_recv.at[q, 0], other_core).start()

        @pl.when(s > 0)
        def _():
            opposite(s - 1, u)

        from_left = piece(row_s, (x + 3) % RING, core, u)
        from_right = piece(row_s, (x + 1) % RING, core, u)
        part = kv.at[0, from_left]
        landed(part, right_recv.at[q, 0])
        remote(part, part, right_send.at[q, 2], right_recv.at[q, 2], right).start()
        part = kv.at[1, from_right]
        landed(part, left_recv.at[q, 1])
        remote(part, part, left_send.at[q, 2], left_recv.at[q, 2], left).start()
        landed(kv.at[1, from_left], right_recv.at[q, 1])
        part = kv.at[:, from_left]
        remote(part, part, core_send.at[q, 1], core_recv.at[q, 1], other_core).start()
        landed(kv.at[0, from_right], left_recv.at[q, 0])
        part = kv.at[:, from_right]
        remote(part, part, core_send.at[q, 2], core_recv.at[q, 2], other_core).start()

    def opposite(s, u):
        far, q = piece(row - s, (x + 2) % RING, core, u), u * RING + s
        landed(kv.at[0, far], right_recv.at[q, 2])
        landed(kv.at[1, far], left_recv.at[q, 2])
        part = kv.at[:, far]
        remote(part, part, core_send.at[q, 3], core_recv.at[q, 3], other_core).start()

    def core_landed(s, carry):
        for u in range(2):
            for n, shift in enumerate((0, 3, 1, 2)):
                landed(
                    kv.at[:, piece(row - s, (x + shift) % RING, 1 - core, u)],
                    core_recv.at[u * RING + s, n],
                )
        return carry

    def weight_step(n):
        from_left, from_right = (y + 3) % RING, (y + 1) % RING
        rows, low, high = half_rows(0, 256), half_rows(0, 128), half_rows(128, 128)
        landed(weight.at[n, from_left, rows], wright_recv.at[n, 0])
        part = weight.at[n, from_left, low]
        remote(part, part, wright_send.at[n, 1], wright_recv.at[n, 1], y_right).start()
        landed(weight.at[n, from_right, rows], wleft_recv.at[n, 0])
        part = weight.at[n, from_right, high]
        remote(part, part, wleft_send.at[n, 1], wleft_recv.at[n, 1], y_left).start()
        for m, source in enumerate((from_left, from_right)):
            part = weight.at[n, source, rows]
            remote(part, part, wcore_send.at[n, m], wcore_recv.at[n, m], other_core).start()

    def weight_far(n):
        far = (y + 2) % RING
        landed(weight.at[n, far, half_rows(0, 128)], wright_recv.at[n, 1])
        landed(weight.at[n, far, half_rows(128, 128)], wleft_recv.at[n, 1])
        part = weight.at[n, far, half_rows(0, 256)]
        remote(part, part, wcore_send.at[n, 2], wcore_recv.at[n, 2], other_core).start()

    def weight_landed(n):
        rows = pl.ds(pl.multiple_of((1 - core) * 256, 256), 256)
        for m, shift in enumerate((3, 1, 2)):
            landed(weight.at[n, (y + shift) % RING, rows], wcore_recv.at[n, m])

    lane = lax.broadcasted_iota(jnp.int32, (1, LANES), 1)
    diagonal_row = lax.broadcasted_iota(jnp.int32, (GROUP * MASK_BLOCK_SIZE, LANES), 0) % MASK_BLOCK_SIZE
    diagonal_lane = lax.broadcasted_iota(jnp.int32, (GROUP * MASK_BLOCK_SIZE, LANES), 1)
    future = (diagonal_lane < MASK_BLOCK_SIZE) & (diagonal_lane > diagonal_row)

    def attend(pair, b):
        block = pair * 2 + b
        blocks, biases = [], []
        for j in range(NV):
            entry = vert[0, j, block]
            blocks.append(jnp.maximum(entry, 0))
            biases.append(jnp.where(entry >= 0, 0.0, NEGATIVE).astype(jnp.float32))
        for j in range(NS):
            entry = slash[0, j, block]
            blocks.append(ctx * 16 + block - jnp.maximum(entry, 0))
            biases.append(jnp.where(entry >= 0, 0.0, NEGATIVE).astype(jnp.float32))
        rows = pl.ds(b * MASK_BLOCK_SIZE, MASK_BLOCK_SIZE)
        query = jnp.concatenate(
            [queries[pair, rows, pl.ds(g * HEAD_SIZE, HEAD_SIZE)] for g in range(GROUP)], axis=0
        )
        keys = jnp.concatenate([kv[0, n] for n in blocks], axis=0)
        scores = lax.dot_general(
            query, keys, (((1,), (1,)), ((), ())), preferred_element_type=jnp.float32
        )
        pieces = []
        for n in range((NV + NS) // 2):
            bias = jnp.where(lane < MASK_BLOCK_SIZE, biases[2 * n], biases[2 * n + 1])
            part = scores[:, n * LANES : (n + 1) * LANES] + bias
            if n == NV // 2:
                part = jnp.where(future, NEGATIVE, part)
            pieces.append(part)
        scores = jnp.concatenate(pieces, axis=1)
        top = jnp.max(scores, axis=-1, keepdims=True)
        weights = jnp.exp2((scores - top) * EXPONENT_SCALE)
        total = jnp.sum(weights, axis=-1, keepdims=True)
        values = jnp.concatenate([kv[1, n] for n in blocks], axis=0)
        out = jnp.dot(weights.astype(jnp.bfloat16), values, preferred_element_type=jnp.float32)
        out = (out / total).astype(jnp.bfloat16)
        for g in range(GROUP):
            mixed[pair, rows, pl.ds(g * HEAD_SIZE, HEAD_SIZE)] = out[
                g * MASK_BLOCK_SIZE : (g + 1) * MASK_BLOCK_SIZE
            ]

    def mix_place(m):
        turn, j = m // RING, m % RING + 1
        token_half = (1 - half) * (1 - turn) + half * turn
        return turn, j, token_half, (y + j) % RING

    def operands_landed():
        lax.fori_loop(0, row + 1, core_landed, 0)
        own_queries().wait()
        for j in range(1, HEADS):
            landed(queries.at[(head + HEADS - j) % HEADS], query_recv.at[j])

    def attention(first, last):
        def pair_step(m, carry):
            turn, j, token_half, target = mix_place(m)
            pair = token_half * RING + target
            for b in range(2):
                attend(pair, b)

            @pl.when(j < RING)
            def _():
                remote(
                    mixed.at[pair], gathered.at[token_half, y],
                    mix_send.at[m], mix_recv.at[m], (ctx, half * RING + target),
                ).start()

            @pl.when(j == RING)
            def _():
                gathered[token_half, y] = mixed[pair]

            return carry

        lax.fori_loop(first, last, pair_step, 0)

    def mix_landed(turn):
        token_half = 1 - half if turn == 0 else half
        for j in range(1, RING):
            landed(gathered.at[token_half, (y + RING - j) % RING], mix_recv.at[turn * RING + j - 1])

    def project(token_half, n, columns):
        total = None
        for source in range(RING):
            term = jnp.dot(
                gathered[token_half, source], weight[n, source, :, columns],
                preferred_element_type=jnp.float32,
            )
            total = term if total is None else total + term
        return total

    def send_part(n, carry):
        weight_landed(n)
        for t in range(CHUNK // 512):
            columns = pl.ds(t * 512, 512)
            outgoing[n, :, columns] = project(1 - half, n, columns).astype(jnp.bfloat16)
        remote(
            outgoing.at[n], incoming.at[n], part_send.at[n], part_recv.at[n], partner
        ).start()
        return carry

    last_row = row == RING - 1

    def first_half(s, carry):
        ctx_step(s, 0)
        first = jnp.where(last_row, jnp.maximum(s - 1, 0), 0)
        last = jnp.where(last_row | (s == row), s, 0)
        lax.fori_loop(first, last, hand_down, 0)
        return carry

    for j in (4, 3, 5, 2, 6, 1, 7):
        query_copy(j).start()
    lax.fori_loop(0, row + 1, first_half, 0)
    own_queries().start()
    for n in range(CHUNKS):
        own_weight(n).start()
    opposite(row, 0)

    def step(s, carry):
        @pl.when(s <= row)
        def _():
            ctx_step(s, 1)

        @pl.when(s < CHUNKS)
        def _():
            weight_step(s)

        @pl.when(s > 0)
        def _():
            weight_far(s - 1)

        @pl.when(s == row)
        def _():
            opposite(s, 1)
            operands_landed()
            attention(0, RING)

        @pl.when(s == row + 1)
        def _():
            for n in range(CHUNKS):
                own_weight(n).wait()
            mix_landed(0)

        first = jnp.where(s == row + 1, 0, s - 1)
        last = jnp.where(s > row, s, first)
        lax.fori_loop(first, last, send_part, 0)
        return carry

    lax.fori_loop(0, CHUNKS + 1, step, 0)

    attention(RING, 2 * RING)
    mix_landed(1)

    def own_part(n, carry):
        for t in range(CHUNK // 512):
            columns = pl.ds(t * 512, 512)
            stream[n, :, columns] = project(half, n, columns)
        return carry

    lax.fori_loop(0, CHUNKS, own_part, 0)

    for n in range(CHUNKS):
        landed(incoming.at[n], part_recv.at[n])
        stream[n] = stream[n] + incoming[n].astype(jnp.float32)

    for j in range(1, HEADS):
        query_copy(j).wait_send()
    for n in range(2):
        for j in range(RING):
            if j > 0:
                near_copy(j, n).wait_send()
            far_copy(j, n).wait_send()

    def down_sent(row_, carry):
        sent(kv.at[:, piece(row_, x, core, 1)], down_send.at[row_])
        return carry

    lax.fori_loop(0, row, down_sent, 0)

    def ctx_sent(s, carry):
        own = kv.at[:, piece(row - s, x, core, 0)]
        part = kv.at[0, piece(row - s, x, core, 0)]

        @pl.when(row < RING - 1)
        def _():
            sent(own, up_send.at[s])

        for u in range(2):
            for n in range(3):
                sent(part, right_send.at[u * RING + s, n])
                sent(part, left_send.at[u * RING + s, n])
            for n in range(4):
                sent(own, core_send.at[u * RING + s, n])
        return carry

    lax.fori_loop(0, row + 1, ctx_sent, 0)

    def weight_sent(n, carry):
        rows, low = half_rows(0, 256), half_rows(0, 128)
        sent(weight.at[n, y, rows], wright_send.at[n, 0])
        sent(weight.at[n, y, rows], wleft_send.at[n, 0])
        sent(weight.at[n, y, low], wright_send.at[n, 1])
        sent(weight.at[n, y, low], wleft_send.at[n, 1])
        for m in range(3):
            sent(weight.at[n, y, rows], wcore_send.at[n, m])
        sent(outgoing.at[n], part_send.at[n])
        return carry

    lax.fori_loop(0, CHUNKS, weight_sent, 0)
    for turn in range(2):
        for j in range(1, RING):
            sent(mixed.at[0], mix_send.at[turn * RING + j - 1])


def finish(stream, residual, gain, hidden_out, normed_out):
    square = jnp.zeros((stream.shape[1], 1), jnp.float32)
    values = []
    for n in range(CHUNKS):
        columns = slice(n * CHUNK, (n + 1) * CHUNK)
        value = stream[n] + residual[:, columns].astype(jnp.float32)
        hidden_out[:, columns] = value.astype(jnp.bfloat16)
        square = square + jnp.sum(value * value, axis=-1, keepdims=True)
        values.append(value)
    scale = lax.rsqrt(square * (1.0 / D) + 1e-05)
    for n in range(D // LANES):
        place = n * LANES % CHUNK
        value = values[n * LANES // CHUNK][:, place : place + LANES]
        normed_out[:, n * LANES : (n + 1) * LANES] = (
            value * scale * gain[n : n + 1].astype(jnp.float32)
        ).astype(jnp.bfloat16)


def per_device(q, k, v, vert, slash, out_weight, residual, norm_gain):
    anywhere = pl.BlockSpec(memory_space=pl.ANY)
    vmem = pl.BlockSpec(memory_space=pltpu.VMEM)
    smem = pl.BlockSpec(memory_space=pltpu.SMEM)
    dma = pltpu.SemaphoreType.DMA
    tokens = q.shape[0]
    stream = pl.pallas_call(
        kernel,
        out_shape=jax.ShapeDtypeStruct((CHUNKS, tokens, CHUNK), jnp.float32),
        in_specs=[anywhere] * 4 + [smem, smem],
        out_specs=vmem,
        scratch_shapes=[
            pltpu.VMEM((2, 512, MASK_BLOCK_SIZE, HEAD_SIZE), jnp.bfloat16),
            pltpu.VMEM((HEADS, tokens, 512), jnp.bfloat16),
            pltpu.VMEM((CHUNKS, RING, 512, CHUNK), jnp.bfloat16),
            pltpu.VMEM((HEADS, tokens, 512), jnp.bfloat16),
            pltpu.VMEM((2, RING, tokens, 512), jnp.bfloat16),
            pltpu.VMEM((CHUNKS, tokens, CHUNK), jnp.bfloat16),
            pltpu.VMEM((CHUNKS, tokens, CHUNK), jnp.bfloat16),
            dma((RING, 2)), dma((RING, 2)), dma((RING, 2)), dma((RING, RING, 2)),
            dma((HEADS,)), dma((HEADS,)),
            dma((RING,)), dma((RING,)), dma((RING,)), dma((RING,)),
            dma((2 * RING, 3)), dma((2 * RING, 3)), dma((2 * RING, 3)), dma((2 * RING, 3)),
            dma((2 * RING, 4)), dma((2 * RING, 4)),
            dma((CHUNKS, 2)), dma((CHUNKS, 2)), dma((CHUNKS, 2)), dma((CHUNKS, 2)),
            dma((CHUNKS, 3)), dma((CHUNKS, 3)),
            dma((2 * RING,)), dma((2 * RING,)), dma((CHUNKS,)), dma((CHUNKS,)),
            dma((3 + CHUNKS,)),
        ],
        compiler_params=pltpu.CompilerParams(
            collective_id=0, has_side_effects=True, vmem_limit_bytes=54 * 1024 * 1024
        ),
        cost_estimate=pl.CostEstimate(
            flops=6_000_000_000, bytes_accessed=10_000_000, transcendentals=3_200_000
        ),
        name="attention_layer",
    )(
        q,
        k.reshape(tokens // MASK_BLOCK_SIZE, MASK_BLOCK_SIZE, -1),
        v.reshape(tokens // MASK_BLOCK_SIZE, MASK_BLOCK_SIZE, -1),
        out_weight, vert.transpose(0, 2, 1), slash.transpose(0, 2, 1),
    )
    rows = 32
    row_block = pl.BlockSpec((rows, D), lambda i: (i, 0))
    return pl.pallas_call(
        finish,
        grid=(tokens // rows,),
        out_shape=[jax.ShapeDtypeStruct((tokens, D), jnp.bfloat16)] * 2,
        in_specs=[
            pl.BlockSpec((CHUNKS, rows, CHUNK), lambda i: (0, i, 0)),
            row_block,
            pl.BlockSpec((D // LANES, LANES), lambda i: (0, 0)),
        ],
        out_specs=[row_block, row_block],
        name="residual_norm",
    )(stream, residual, norm_gain.reshape(D // LANES, LANES))


def solution(mesh):
    token_rows = P(("ctx", "head"), None)
    return jax.shard_map(
        lambda *args: tuple(per_device(*args)),
        mesh=mesh,
        in_specs=(
            token_rows, token_rows, token_rows,
            P("head", "ctx", None), P("head", "ctx", None),
            P("head", None), token_rows, P(),
        ),
        out_specs=(token_rows, token_rows),
        check_vma=False,
    )
```

```python
import functools

import jax
import jax.numpy as jnp
from jax import lax
from jax.experimental import pallas as pl
from jax.experimental.pallas import tpu as pltpu
from jax.sharding import PartitionSpec as P

MESH = pl.DeviceIdType.MESH
HEAD_SIZE = 128
MASK_BLOCK_SIZE = 64
LANES = 128
GROUP = 4
NV = 8
NS = 4
RING = 4
HEADS = 8
CHUNKS = 4
D = 4096
CHUNK = D // CHUNKS
NEGATIVE = -1e30
EXPONENT_SCALE = HEAD_SIZE**-0.5 * 1.4426950408889634


def kernel(
    q_in, k_in, v_in, w_in, vert, slash,
    stream,
    kv, queries, weight, mixed, gathered, outgoing, incoming,
    near_send, near_recv, far_send, far_recv, query_send, query_recv,
    up_send, up_recv, down_send, down_recv,
    right_send, right_recv, left_send, left_recv, core_send, core_recv,
    wright_send, wright_recv, wleft_send, wleft_recv, wcore_send, wcore_recv,
    mix_send, mix_recv, part_send, part_recv, local_sem,
):
    ctx = lax.axis_index("ctx")
    head = lax.axis_index("head")
    core, x, row = ctx % 2, (ctx // 2) % RING, ctx // (2 * RING)
    y, half = head % RING, head // RING

    def at_ctx(row_, x_, core_):
        return ((row_ * RING + x_) * 2 + core_, head)

    right = at_ctx(row, (x + 1) % RING, core)
    left = at_ctx(row, (x + 3) % RING, core)
    other_core = at_ctx(row, x, 1 - core)
    up = at_ctx((row + 1) % RING, x, core)
    down = at_ctx((row + 3) % RING, x, core)
    y_right = (ctx, half * RING + (y + 1) % RING)
    y_left = (ctx, half * RING + (y + 3) % RING)
    partner = (ctx, (1 - half) * RING + y)

    def head_peer(j):
        return (ctx, (head + j) % HEADS)

    def remote(src, dst, send, recv, device):
        return pltpu.make_async_remote_copy(
            src_ref=src, dst_ref=dst, send_sem=send, recv_sem=recv,
            device_id=device, device_id_type=MESH,
        )

    def landed(dst, recv):
        remote(dst, dst, recv, recv, other_core).wait_recv()

    def sent(src, send):
        remote(src, src, send, send, other_core).wait_send()

    def far_peer(row_, y_):
        return ((row_ * RING + x) * 2 + core, (1 - half) * RING + y_)

    barrier = pltpu.get_barrier_semaphore()
    friends = [head_peer(j) for j in range(1, HEADS)] + [right, left, other_core, up, down]
    for friend in friends:
        pl.semaphore_signal(barrier, inc=1, device_id=friend, device_id_type=MESH)

    @pl.when(row == RING - 1)
    def _():
        for row_ in range(RING - 1):
            for y_ in range(RING):
                pl.semaphore_signal(
                    barrier, inc=1, device_id=far_peer(row_, y_), device_id_type=MESH
                )

    def own_rows(n):
        return pltpu.make_async_copy(
            (k_in, v_in)[n].at[:, :, pl.ds(pl.multiple_of(head * LANES, LANES), LANES)],
            kv.at[n, pl.ds(ctx * 16 + head * 2, 2)],
            local_sem.at[n],
        )

    def own_queries():
        return pltpu.make_async_copy(
            q_in.at[:, pl.ds(pl.multiple_of(head * 512, 512), 512)],
            queries.at[head],
            local_sem.at[2],
        )

    def own_weight(n):
        return pltpu.make_async_copy(
            w_in.at[:, pl.ds(n * CHUNK, CHUNK)], weight.at[n, y], local_sem.at[3 + n]
        )

    own_rows(0).start()
    own_rows(1).start()
    pl.semaphore_wait(barrier, len(friends) + jnp.where(row < RING - 1, RING, 0))

    def key_value_copy(n, target, send, recv, device):
        src = (k_in, v_in)[n]
        return remote(
            src.at[:, :, pl.ds(pl.multiple_of(target * LANES, LANES), LANES)],
            kv.at[n, pl.ds(ctx * 16 + head * 2, 2)], send, recv, device,
        )

    def near_copy(j, n):
        target = half * RING + (y + j) % RING
        return key_value_copy(n, target, near_send.at[j, n], near_recv.at[j, n], (ctx, target))

    def far_copy(j, n):
        y_ = (y + j) % RING
        device = far_peer(RING - 1, y_)
        return key_value_copy(
            n, device[1], far_send.at[j, n], far_recv.at[row, j, n], device
        )

    def query_copy(j):
        peer = head_peer(j)
        return remote(
            q_in.at[:, pl.ds(pl.multiple_of(peer[1] * 512, 512), 512)],
            queries.at[head],
            query_send.at[j], query_recv.at[j], peer,
        )

    for j in (1, 3, 2):
        for n in range(2):
            near_copy(j, n).start()
    for j in range(RING):
        for n in range(2):
            far_copy(j, n).start()

    def piece(row_, x_, core_, u):
        owner = half if u == 0 else 1 - half
        return pl.ds(((row_ * RING + x_) * 2 + core_) * 16 + owner * 8, 8)

    def far_landed(row_):
        @pl.when(row == RING - 1)
        def _():
            for j in range(RING):
                source = (1 - half) * RING + (y + RING - j) % RING
                place = pl.ds(((row_ * RING + x) * 2 + core) * 16 + source * 2, 2)
                for n in range(2):
                    landed(kv.at[n, place], far_recv.at[row_, j, n])

        @pl.when(row < RING - 1)
        def _():
            landed(kv.at[:, piece(row_, x, core, 1)], down_recv.at[row_])

    def hand_down(row_, carry):
        far_landed(row_)
        part = kv.at[:, piece(row_, x, core, 1)]
        remote(part, part, down_send.at[row_], down_recv.at[row_], down).start()
        return carry

    def half_rows(start, count):
        return pl.ds(pl.multiple_of(core * 256 + start, 128), count)

    def weight_first(n):
        rows = half_rows(0, 256)
        src = w_in.at[rows, pl.ds(n * CHUNK, CHUNK)]
        dst = weight.at[n, y, rows]
        remote(src, dst, wright_send.at[n, 0], wright_recv.at[n, 0], y_right).start()
        remote(src, dst, wleft_send.at[n, 0], wleft_recv.at[n, 0], y_left).start()

    for n in range(CHUNKS):
        weight_first(n)

    def ctx_step(s, u):
        row_s = row - s
        q = u * RING + s
        own = kv.at[:, piece(row_s, x, core, u)]
        if u == 0:
            @pl.when(s == 0)
            def _():
                for n in range(2):
                    own_rows(n).wait()
                for j in range(1, RING):
                    source = half * RING + (y + RING - j) % RING
                    for n in range(2):
                        landed(kv.at[n, pl.ds(ctx * 16 + source * 2, 2)], near_recv.at[j, n])

            @pl.when(s > 0)
            def _():
                landed(own, up_recv.at[s])

            @pl.when(row < RING - 1)
            def _():
                remote(own, own, up_send.at[s], up_recv.at[s + 1], up).start()
        else:
            @pl.when(s == 0)
            def _():
                far_landed(row)

        for n in (0, 1):
            def to_right(n=n):
                part = kv.at[n, piece(row_s, x, core, u)]
                remote(part, part, right_send.at[q, n], right_recv.at[q, n], right).start()

            def to_left(n=n):
                part = kv.at[1 - n, piece(row_s, x, core, u)]
                remote(part, part, left_send.at[q, 1 - n], left_recv.at[q, 1 - n], left).start()

            pl.when((s > 0) | (x < 3))(to_right)
            pl.when((s > 0) | (x == 0) | ((x == 1) & (n == 0)))(to_left)
        remote(own, own, core_send.at[q, 0], core_recv.at[q, 0], other_core).start()

        @pl.when(s > 0)
        def _():
            opposite(s - 1, u)

        from_left = piece(row_s, (x + 3) % RING, core, u)
        from_right = piece(row_s, (x + 1) % RING, core, u)
        def k_from_left():
            landed(kv.at[0, from_left], right_recv.at[q, 0])

        def k_to_right():
            part = kv.at[0, from_left]
            remote(part, part, right_send.at[q, 2], right_recv.at[q, 2], right).start()

        def v_from_right():
            part = kv.at[1, from_right]
            landed(part, left_recv.at[q, 1])
            remote(part, part, left_send.at[q, 2], left_recv.at[q, 2], left).start()

        def left_to_core():
            landed(kv.at[1, from_left], right_recv.at[q, 1])
            part = kv.at[:, from_left]
            remote(part, part, core_send.at[q, 1], core_recv.at[q, 1], other_core).start()

        def right_to_core():
            landed(kv.at[0, from_right], left_recv.at[q, 0])
            part = kv.at[:, from_right]
            remote(part, part, core_send.at[q, 2], core_recv.at[q, 2], other_core).start()

        pl.when((s > 0) | (x > 0))(k_from_left)
        pl.when((s > 0) | (x == 1) | (x == 2))(k_to_right)
        pl.when((s > 0) | (x == 3) | (x == 0))(v_from_right)
        pl.when((s > 0) | (x > 0))(left_to_core)
        pl.when((s > 0) | (x == 3))(right_to_core)

    def opposite(s, u):
        far, q = piece(row - s, (x + 2) % RING, core, u), u * RING + s

        @pl.when((s > 0) | (x > 1))
        def _():
            landed(kv.at[0, far], right_recv.at[q, 2])
            landed(kv.at[1, far], left_recv.at[q, 2])
            part = kv.at[:, far]
            remote(part, part, core_send.at[q, 3], core_recv.at[q, 3], other_core).start()

    def from_core(s, n):
        return (s > 0) | (x >= (0, 1, 3, 2)[n])

    def core_landed(s, carry):
        for u in range(2):
            for n, shift in enumerate((0, 3, 1, 2)):
                @pl.when(from_core(s, n))
                def _():
                    landed(
                        kv.at[:, piece(row - s, (x + shift) % RING, 1 - core, u)],
                        core_recv.at[u * RING + s, n],
                    )
        return carry

    def weight_step(n):
        from_left, from_right = (y + 3) % RING, (y + 1) % RING
        rows, low, high = half_rows(0, 256), half_rows(0, 128), half_rows(128, 128)
        landed(weight.at[n, from_left, rows], wright_recv.at[n, 0])
        part = weight.at[n, from_left, low]
        remote(part, part, wright_send.at[n, 1], wright_recv.at[n, 1], y_right).start()
        landed(weight.at[n, from_right, rows], wleft_recv.at[n, 0])
        part = weight.at[n, from_right, high]
        remote(part, part, wleft_send.at[n, 1], wleft_recv.at[n, 1], y_left).start()
        for m, source in enumerate((from_left, from_right)):
            part = weight.at[n, source, rows]
            remote(part, part, wcore_send.at[n, m], wcore_recv.at[n, m], other_core).start()

    def weight_far(n):
        far = (y + 2) % RING
        landed(weight.at[n, far, half_rows(0, 128)], wright_recv.at[n, 1])
        landed(weight.at[n, far, half_rows(128, 128)], wleft_recv.at[n, 1])
        part = weight.at[n, far, half_rows(0, 256)]
        remote(part, part, wcore_send.at[n, 2], wcore_recv.at[n, 2], other_core).start()

    def weight_landed(n):
        rows = pl.ds(pl.multiple_of((1 - core) * 256, 256), 256)
        for m, shift in enumerate((3, 1, 2)):
            landed(weight.at[n, (y + shift) % RING, rows], wcore_recv.at[n, m])

    lane = lax.broadcasted_iota(jnp.int32, (1, LANES), 1)
    diagonal_row = lax.broadcasted_iota(jnp.int32, (GROUP * MASK_BLOCK_SIZE, LANES), 0) % MASK_BLOCK_SIZE
    diagonal_lane = lax.broadcasted_iota(jnp.int32, (GROUP * MASK_BLOCK_SIZE, LANES), 1)
    future = (diagonal_lane < MASK_BLOCK_SIZE) & (diagonal_lane > diagonal_row)

    def attend(pair, b):
        block = pair * 2 + b
        blocks, biases = [], []
        for j in range(NV):
            entry = vert[0, j, block]
            blocks.append(jnp.maximum(entry, 0))
            biases.append(jnp.where(entry >= 0, 0.0, NEGATIVE).astype(jnp.float32))
        for j in range(NS):
            entry = slash[0, j, block]
            blocks.append(ctx * 16 + block - jnp.maximum(entry, 0))
            biases.append(jnp.where(entry >= 0, 0.0, NEGATIVE).astype(jnp.float32))
        rows = pl.ds(b * MASK_BLOCK_SIZE, MASK_BLOCK_SIZE)
        query = jnp.concatenate(
            [queries[pair, rows, pl.ds(g * HEAD_SIZE, HEAD_SIZE)] for g in range(GROUP)], axis=0
        )
        keys = jnp.concatenate([kv[0, n] for n in blocks], axis=0)
        scores = lax.dot_general(
            query, keys, (((1,), (1,)), ((), ())), preferred_element_type=jnp.float32
        )
        pieces = []
        for n in range((NV + NS) // 2):
            bias = jnp.where(lane < MASK_BLOCK_SIZE, biases[2 * n], biases[2 * n + 1])
            part = scores[:, n * LANES : (n + 1) * LANES] + bias
            if n == NV // 2:
                part = jnp.where(future, NEGATIVE, part)
            pieces.append(part)
        scores = jnp.concatenate(pieces, axis=1)
        top = jnp.max(scores, axis=-1, keepdims=True)
        weights = jnp.exp2((scores - top) * EXPONENT_SCALE)
        total = jnp.sum(weights, axis=-1, keepdims=True)
        values = jnp.concatenate([kv[1, n] for n in blocks], axis=0)
        out = jnp.dot(weights.astype(jnp.bfloat16), values, preferred_element_type=jnp.float32)
        out = (out / total).astype(jnp.bfloat16)
        for g in range(GROUP):
            mixed[pair, rows, pl.ds(g * HEAD_SIZE, HEAD_SIZE)] = out[
                g * MASK_BLOCK_SIZE : (g + 1) * MASK_BLOCK_SIZE
            ]

    def mix_place(m):
        turn, j = m // RING, m % RING + 1
        token_half = (1 - half) * (1 - turn) + half * turn
        return turn, j, token_half, (y + j) % RING

    def operands_landed():
        lax.fori_loop(0, row + 1, core_landed, 0)
        own_queries().wait()
        for j in range(1, HEADS):
            landed(queries.at[(head + HEADS - j) % HEADS], query_recv.at[j])

    def attention(first, last):
        def pair_step(m, carry):
            turn, j, token_half, target = mix_place(m)
            pair = token_half * RING + target
            for b in range(2):
                attend(pair, b)

            @pl.when(j < RING)
            def _():
                remote(
                    mixed.at[pair], gathered.at[token_half, y],
                    mix_send.at[m], mix_recv.at[m], (ctx, half * RING + target),
                ).start()

            @pl.when(j == RING)
            def _():
                gathered[token_half, y] = mixed[pair]

            return carry

        lax.fori_loop(first, last, pair_step, 0)

    def mix_landed(turn):
        token_half = 1 - half if turn == 0 else half
        for j in range(1, RING):
            landed(gathered.at[token_half, (y + RING - j) % RING], mix_recv.at[turn * RING + j - 1])

    def project(token_half, n, columns):
        total = None
        for source in range(RING):
            term = jnp.dot(
                gathered[token_half, source], weight[n, source, :, columns],
                preferred_element_type=jnp.float32,
            )
            total = term if total is None else total + term
        return total

    def send_part(n, carry):
        weight_landed(n)
        for t in range(CHUNK // 512):
            columns = pl.ds(t * 512, 512)
            outgoing[n, :, columns] = project(1 - half, n, columns).astype(jnp.bfloat16)
        remote(
            outgoing.at[n], incoming.at[n], part_send.at[n], part_recv.at[n], partner
        ).start()
        return carry

    last_row = row == RING - 1

    def first_half(s, carry):
        ctx_step(s, 0)
        first = jnp.where(last_row, jnp.maximum(s - 1, 0), 0)
        last = jnp.where(last_row | (s == row), s, 0)
        lax.fori_loop(first, last, hand_down, 0)
        return carry

    for j in (4, 3, 5, 2, 6, 1, 7):
        query_copy(j).start()
    lax.fori_loop(0, row + 1, first_half, 0)
    own_queries().start()
    for n in range(CHUNKS):
        own_weight(n).start()
    opposite(row, 0)

    def step(s, carry):
        @pl.when(s <= row)
        def _():
            ctx_step(s, 1)

        @pl.when(s < CHUNKS)
        def _():
            weight_step(s)

        @pl.when(s > 0)
        def _():
            weight_far(s - 1)

        @pl.when(s == row)
        def _():
            opposite(s, 1)
            operands_landed()
            attention(0, RING)

        @pl.when(s == row + 1)
        def _():
            for n in range(CHUNKS):
                own_weight(n).wait()
            mix_landed(0)

        first = jnp.where(s == row + 1, 0, s - 1)
        last = jnp.where(s > row, s, first)
        lax.fori_loop(first, last, send_part, 0)
        return carry

    lax.fori_loop(0, CHUNKS + 1, step, 0)

    attention(RING, 2 * RING)
    mix_landed(1)

    def own_part(n, carry):
        for t in range(CHUNK // 512):
            columns = pl.ds(t * 512, 512)
            stream[n, :, columns] = project(half, n, columns)
        return carry

    lax.fori_loop(0, CHUNKS, own_part, 0)

    for n in range(CHUNKS):
        landed(incoming.at[n], part_recv.at[n])
        stream[n] = stream[n] + incoming[n].astype(jnp.float32)

    for j in range(1, HEADS):
        query_copy(j).wait_send()
    for n in range(2):
        for j in range(RING):
            if j > 0:
                near_copy(j, n).wait_send()
            far_copy(j, n).wait_send()

    def down_sent(row_, carry):
        sent(kv.at[:, piece(row_, x, core, 1)], down_send.at[row_])
        return carry

    lax.fori_loop(0, row, down_sent, 0)

    def ctx_sent(s, carry):
        own = kv.at[:, piece(row - s, x, core, 0)]
        part = kv.at[0, piece(row - s, x, core, 0)]

        @pl.when(row < RING - 1)
        def _():
            sent(own, up_send.at[s])

        for u in range(2):
            for n in range(3):
                to_right = (s > 0) | ((x == 1) | (x == 2) if n == 2 else x < 3)
                to_left = (s > 0) | (x == 0) | (
                    x == 3 if n == 2 else (x == 1) & (n == 1)
                )
                pl.when(to_right)(lambda: sent(part, right_send.at[u * RING + s, n]))
                pl.when(to_left)(lambda: sent(part, left_send.at[u * RING + s, n]))
            for n in range(4):
                pl.when(from_core(s, n))(lambda: sent(own, core_send.at[u * RING + s, n]))
        return carry

    lax.fori_loop(0, row + 1, ctx_sent, 0)

    def weight_sent(n, carry):
        rows, low = half_rows(0, 256), half_rows(0, 128)
        sent(weight.at[n, y, rows], wright_send.at[n, 0])
        sent(weight.at[n, y, rows], wleft_send.at[n, 0])
        sent(weight.at[n, y, low], wright_send.at[n, 1])
        sent(weight.at[n, y, low], wleft_send.at[n, 1])
        for m in range(3):
            sent(weight.at[n, y, rows], wcore_send.at[n, m])
        sent(outgoing.at[n], part_send.at[n])
        return carry

    lax.fori_loop(0, CHUNKS, weight_sent, 0)
    for turn in range(2):
        for j in range(1, RING):
            sent(mixed.at[0], mix_send.at[turn * RING + j - 1])


def finish(stream, residual, gain, hidden_out, normed_out):
    square = jnp.zeros((stream.shape[1], 1), jnp.float32)
    values = []
    for n in range(CHUNKS):
        columns = slice(n * CHUNK, (n + 1) * CHUNK)
        value = stream[n] + residual[:, columns].astype(jnp.float32)
        hidden_out[:, columns] = value.astype(jnp.bfloat16)
        square = square + jnp.sum(value * value, axis=-1, keepdims=True)
        values.append(value)
    scale = lax.rsqrt(square * (1.0 / D) + 1e-05)
    for n in range(D // LANES):
        place = n * LANES % CHUNK
        value = values[n * LANES // CHUNK][:, place : place + LANES]
        normed_out[:, n * LANES : (n + 1) * LANES] = (
            value * scale * gain[n : n + 1].astype(jnp.float32)
        ).astype(jnp.bfloat16)


def per_device(q, k, v, vert, slash, out_weight, residual, norm_gain):
    anywhere = pl.BlockSpec(memory_space=pl.ANY)
    vmem = pl.BlockSpec(memory_space=pltpu.VMEM)
    smem = pl.BlockSpec(memory_space=pltpu.SMEM)
    dma = pltpu.SemaphoreType.DMA
    tokens = q.shape[0]
    stream = pl.pallas_call(
        kernel,
        out_shape=jax.ShapeDtypeStruct((CHUNKS, tokens, CHUNK), jnp.float32),
        in_specs=[anywhere] * 4 + [smem, smem],
        out_specs=vmem,
        scratch_shapes=[
            pltpu.VMEM((2, 512, MASK_BLOCK_SIZE, HEAD_SIZE), jnp.bfloat16),
            pltpu.VMEM((HEADS, tokens, 512), jnp.bfloat16),
            pltpu.VMEM((CHUNKS, RING, 512, CHUNK), jnp.bfloat16),
            pltpu.VMEM((HEADS, tokens, 512), jnp.bfloat16),
            pltpu.VMEM((2, RING, tokens, 512), jnp.bfloat16),
            pltpu.VMEM((CHUNKS, tokens, CHUNK), jnp.bfloat16),
            pltpu.VMEM((CHUNKS, tokens, CHUNK), jnp.bfloat16),
            dma((RING, 2)), dma((RING, 2)), dma((RING, 2)), dma((RING, RING, 2)),
            dma((HEADS,)), dma((HEADS,)),
            dma((RING,)), dma((RING,)), dma((RING,)), dma((RING,)),
            dma((2 * RING, 3)), dma((2 * RING, 3)), dma((2 * RING, 3)), dma((2 * RING, 3)),
            dma((2 * RING, 4)), dma((2 * RING, 4)),
            dma((CHUNKS, 2)), dma((CHUNKS, 2)), dma((CHUNKS, 2)), dma((CHUNKS, 2)),
            dma((CHUNKS, 3)), dma((CHUNKS, 3)),
            dma((2 * RING,)), dma((2 * RING,)), dma((CHUNKS,)), dma((CHUNKS,)),
            dma((3 + CHUNKS,)),
        ],
        compiler_params=pltpu.CompilerParams(
            collective_id=0, has_side_effects=True, vmem_limit_bytes=54 * 1024 * 1024
        ),
        cost_estimate=pl.CostEstimate(
            flops=6_000_000_000, bytes_accessed=10_000_000, transcendentals=3_200_000
        ),
        name="attention_layer",
    )(
        q,
        k.reshape(tokens // MASK_BLOCK_SIZE, MASK_BLOCK_SIZE, -1),
        v.reshape(tokens // MASK_BLOCK_SIZE, MASK_BLOCK_SIZE, -1),
        out_weight, vert.transpose(0, 2, 1), slash.transpose(0, 2, 1),
    )
    rows = 16
    row_block = pl.BlockSpec((rows, D), lambda i: (i, 0))
    return pl.pallas_call(
        finish,
        grid=(tokens // rows,),
        out_shape=[jax.ShapeDtypeStruct((tokens, D), jnp.bfloat16)] * 2,
        in_specs=[
            pl.BlockSpec((CHUNKS, rows, CHUNK), lambda i: (0, i, 0)),
            row_block,
            pl.BlockSpec((D // LANES, LANES), lambda i: (0, 0)),
        ],
        out_specs=[row_block, row_block],
        name="residual_norm",
    )(stream, residual, norm_gain.reshape(D // LANES, LANES))


def solution(mesh):
    token_rows = P(("ctx", "head"), None)
    return jax.shard_map(
        lambda *args: tuple(per_device(*args)),
        mesh=mesh,
        in_specs=(
            token_rows, token_rows, token_rows,
            P("head", "ctx", None), P("head", "ctx", None),
            P("head", None), token_rows, P(),
        ),
        out_specs=(token_rows, token_rows),
        check_vma=False,
    )
```
